256 devices in a mesh: dp: 32 (over x, y, z_hi), mp: 8 (over z_lo, core).
Axes of the slice: x: 4, y: 4, z: 8 (z_hi: 2, z_lo: 4; z = z_hi * 4 + z_lo), core: 2. Of those that a mesh axis runs over, the one named last changes fastest.
Arguments:
- activations: bfloat16 [16384, 8192], P('dp'), may hold values from -6 to 6
- cotangent: bfloat16 [16384, 2, 1024], P('dp', None, 'mp'), may hold values from -6 to 6
- param_shard: bfloat16 [8192, 2, 1024], P('dp', None, 'mp'), may hold values from -0.0625 to 0.0625
- master_store: float32 [8192, 2, 1024], P('dp', None, 'mp'), may hold values from -0.0625 to 0.0625
- first_store: float32 [8192, 2, 1024], P('dp', None, 'mp'), may hold values from -768 to 768
- second_store: float32 [8192, 2, 1024], P('dp', None, 'mp'), may hold values from 1024 to 32768
Outputs:
- input_grad: bfloat16 [16384, 8192], P('dp', 'mp')
- new_master: float32 [8192, 2, 1024], P('dp', None, 'mp')
- new_first: float32 [8192, 2, 1024], P('dp', None, 'mp')
- new_second: float32 [8192, 2, 1024], P('dp', None, 'mp')
- new_layer: bfloat16 [8192, 2, 1024], P(None, None, 'mp')
The draws below stay inside these ranges and needn't reach their ends.
All inputs are finite; a program needn't handle non-finite values.
Results may differ from the reference program's by a relative error of at most 0.0075.
Values may be sent and summed in bfloat16 or wider, within the bound.
No kernel may reach another device: no remote copies, remote signals or barrier semaphores. Data moves between devices by JAX's collectives and lax.ppermute only.
A program may use at most 128 MiB of HBM per device.

```python
import math
import jax
import jax.numpy as jnp

D = 8192
KVH = 8
HD = 128
TOKENS = 16384
N_DP = 32


def levels(key, shape, shards, low, high):
    gain, own = 1.0, jax.random.fold_in(key, 6)
    for axis_at, parts in shards:
        heights = jnp.exp(jax.random.uniform(jax.random.fold_in(own, axis_at), (parts,), jnp.float32, low / len(shards), high / len(shards)))
        gain = gain * jnp.repeat(heights, shape[axis_at] // parts).reshape([-1 if axis == axis_at else 1 for axis in range(len(shape))])
    return gain


def gaussian(stream_key, dims, scale, bound, pieces=(), dtype=jnp.bfloat16):
    drawn = scale * jax.random.normal(stream_key, dims, jnp.float32)
    if pieces:
        drawn = drawn * levels(stream_key, dims, pieces, -0.22, 0.18)
    return jnp.clip(drawn, -bound, bound).astype(dtype)


def setup_inputs(seed: int = 0) -> dict:
    arg_keys = jax.random.split(jax.random.key(seed), 7)
    activations = gaussian(arg_keys[0], (TOKENS, D), 1.0, 6.0, ((0, 32),))
    cotangent = gaussian(arg_keys[1], (TOKENS, 2, KVH * HD), 1.0, 6.0, ((0, 32), (2, 8)))
    param_shard = gaussian(arg_keys[2], (D, 2, KVH * HD), D ** -0.5, 0.0625, ((0, 32), (2, 8)))
    master_store = gaussian(arg_keys[3], (D, 2, KVH * HD), D ** -0.5, 0.0625, ((0, 32), (2, 8)), jnp.float32)
    first_store = gaussian(arg_keys[4], (D, 2, KVH * HD), (TOKENS ** 0.5), 768.0, ((0, 32), (2, 8)), jnp.float32)
    second_store = jnp.clip(jnp.exp(math.log(32768.0) - 3.465736 * jax.random.uniform(arg_keys[5], (D, 2, KVH * HD), jnp.float32) ** levels(arg_keys[5], (D, 2, KVH * HD), ((0, 32), (2, 8)), -0.2, 0.2)), 1024.0, 32768.0)
    return dict(activations=activations, cotangent=cotangent, param_shard=param_shard, master_store=master_store, first_store=first_store, second_store=second_store)


learn_rate = 0.001
beta_one = 0.9
beta_two = 0.95
decay_rate = 0.1
epsilon = 1e-08
step_number = 10

def reference(activations, cotangent, param_shard, master_store, first_store, second_store):
    flat_cot = cotangent.reshape(TOKENS, 2 * KVH * HD)
    flat_par = param_shard.reshape(D, 2 * KVH * HD)
    input_grad = jnp.dot(flat_cot, flat_par.T, preferred_element_type=jnp.float32).astype(jnp.bfloat16)
    weight_grad = jnp.dot(activations.T, flat_cot, preferred_element_type=jnp.float32).reshape(D, 2, KVH * HD)
    shard_rows = D // N_DP
    master = jnp.roll(master_store, -shard_rows, axis=0)
    first = jnp.roll(first_store, -shard_rows, axis=0)
    second = jnp.roll(second_store, -shard_rows, axis=0)
    new_first = beta_one * first + (1.0 - beta_one) * weight_grad
    new_second = beta_two * second + (1.0 - beta_two) * weight_grad * weight_grad
    first_hat = new_first / (1.0 - beta_one ** step_number)
    second_hat = new_second / (1.0 - beta_two ** step_number)
    new_master = master - learn_rate * (first_hat / (jnp.sqrt(second_hat) + epsilon) + decay_rate * master)
    new_layer = new_master.astype(jnp.bfloat16)
    return (input_grad, new_master, new_first, new_second, new_layer)
```

```python
import functools

import jax
import jax.numpy as jnp
import numpy as np
from jax import lax
from jax.experimental import pallas as pl
from jax.experimental.pallas import tpu as pltpu
from jax.sharding import Mesh, PartitionSpec as P

learn_rate = 0.001
beta_one = 0.9
beta_two = 0.95
decay_rate = 0.1
epsilon = 1e-08
step_number = 10

SIZES = {"x": 4, "y": 4, "h": 2, "l": 4, "c": 2}
AXES = tuple(SIZES)
DP = ("x", "y", "h")
MP = ("l", "c")
MOST = pltpu.CompilerParams(vmem_limit_bytes=56 * 2**20)
WIDE = pltpu.CompilerParams(vmem_limit_bytes=32 * 2**20)


def move(value, target):
    shape = tuple(SIZES.values())
    pairs = []
    for source in range(int(np.prod(shape))):
        at = dict(zip(AXES, (int(i) for i in np.unravel_index(source, shape))))
        to = target(**at)
        pairs.append((source, int(np.ravel_multi_index([to[a] % SIZES[a] for a in AXES], shape))))
    return lax.ppermute(value, AXES, pairs)


def along_first(by):
    def target(x, y, h, l, c):
        return dict(x=x + by * (1 - c), y=y + by * c, h=h, l=l, c=c)

    return target


def along_second(by):
    def target(x, y, h, l, c):
        return dict(x=x + by * c, y=y + by * (1 - c), h=h, l=l, c=c)

    return target


def other_half(x, y, h, l, c):
    return dict(x=x, y=y, h=h + 1, l=l, c=c)


def other_core(x, y, h, l, c):
    return dict(x=x, y=y, h=h, l=l, c=c + 1)


def next_in_line(x, y, h, l, c):
    return dict(x=x, y=y, h=h, l=l + 1, c=c)


def back_in_line(x, y, h, l, c):
    return dict(x=x, y=y, h=h, l=l - 1, c=c)


def previous_block(x, y, h, l, c):
    block = (x * 8 + y * 2 + h - 1) % 32
    return dict(x=block // 8, y=block // 2 % 4, h=block % 2, l=l, c=c)


def to_user(x, y, h, l, c):
    return dict(x=l, y=2 * c + y % 2, h=h, l=x, c=y // 2)


def to_user_across(x, y, h, l, c):
    return dict(to_user(x, y, h, l, c), h=h + 1)


def pair_at(here, first, second):
    x, y, c = here[0], here[1], here[4]
    first, second = (x + c * (y - x) + first) % 4, (y + c * (x - y) + second) % 4
    return 4 * (first + c * (second - first)) + second + c * (first - second)


def block_at(here, first, second, s, blocks):
    return (2 * pair_at(here, first, second) + blocks - 1 + s) % blocks


def fetch(here, activations, held, sems, g, first, second, s):
    rows = held.shape[2] // 2
    block = block_at(here, first, second, s, activations.shape[1] // rows)
    return pltpu.make_async_copy(
        activations.at[:, pl.ds(pl.multiple_of(block * rows, rows), rows)],
        held.at[g, :, pl.ds(s * rows, rows)],
        sems.at[g, s],
    )


def fetch_all(groups, here, activations, held, sems):
    g = 0
    for first, second, count in groups:
        for i in range(count):
            for s in range(2):
                fetch(here, activations, held, sems, g, first, second + i, s).start()
            g += 1


def multiply_all(groups, here, cot, activations, outs, held, sems, received=()):
    rows = held.shape[2] // 2
    done = 0
    for n, (first, second, count) in enumerate(groups):
        out = outs[n // 2] if received else outs[n]
        base = 2 * (n % 2) if received else 0
        got = received[n // 2] if received and n in (0, 3) else None

        def step(i, carry, out=out, base=base, got=got, done=done, first=first, second=second):
            for s in range(2):
                fetch(here, activations, held, sems, done + i, first, second + i, s).wait()
            both = jnp.dot(cot[...], held[done + i], preferred_element_type=jnp.float32)
            for s in range(2):
                term = both[:, s * rows : (s + 1) * rows]
                if got is not None:
                    term += got[i, here[2] ^ s].astype(jnp.float32)
                out[base + i, here[2] ^ s] = term.astype(out.dtype)
            return carry

        lax.fori_loop(0, count, step, 0)
        done += count


def first_kernel(groups, here, cot_in, par_in, activations, *refs):
    cot, cot_t, par_t, *outs = refs[: 3 + len(groups)]
    held, sems, cot_raw, par_raw, raw_sems, wide = refs[3 + len(groups) :]
    raw = (
        pltpu.make_async_copy(cot_in, cot_raw, raw_sems.at[0]),
        pltpu.make_async_copy(par_in, par_raw, raw_sems.at[1]),
    )
    raw[0].start()
    fetch_all(groups, here, activations, held, sems)
    raw[1].start()
    for copy, source, plain, turned in ((raw[0], cot_raw, cot, cot_t), (raw[1], par_raw, None, par_t)):
        copy.wait()
        rows, width = source.shape[0] // 2, source.shape[1]
        wide[: 2 * rows, :] = source[...].astype(jnp.float32)
        for j in range(2):
            part = wide[pl.ds(j, rows, stride=2), :]
            at = slice(j * width, (j + 1) * width)
            if plain is not None:
                plain[:, at] = part.astype(plain.dtype)
            turned[at, :] = part.T.astype(turned.dtype)
    multiply_all(groups, here, cot_t, activations, outs, held, sems)


def first_terms(here, groups, cotangent, param_shard, activations):
    tokens, rows = cotangent.shape[0], param_shard.shape[0]
    width = cotangent.shape[2]
    total = sum(count for _, _, count in groups)
    any_space = pl.BlockSpec(memory_space=pl.ANY)
    shapes = [(tokens, 2 * width), (2 * width, tokens), (2 * width, rows)]
    shapes += [(count, 2, 2 * width, rows) for _, _, count in groups]
    return pl.pallas_call(
        functools.partial(first_kernel, groups),
        out_shape=[jax.ShapeDtypeStruct(shape, jnp.bfloat16) for shape in shapes],
        in_specs=[pl.BlockSpec(memory_space=pltpu.SMEM), any_space, any_space, any_space],
        scratch_shapes=[
            pltpu.VMEM((total, tokens, 2 * rows), jnp.bfloat16),
            pltpu.SemaphoreType.DMA((total, 2)),
            pltpu.VMEM((2 * tokens, width), jnp.bfloat16),
            pltpu.VMEM((2 * rows, width), jnp.bfloat16),
            pltpu.SemaphoreType.DMA((2,)),
            pltpu.VMEM((2 * max(tokens, rows), width), jnp.float32),
        ],
        compiler_params=MOST,
        cost_estimate=pl.CostEstimate(
            flops=8 * total * width * tokens * rows,
            bytes_accessed=4 * total * rows * (tokens + 2 * width) + 12 * width * tokens,
            transcendentals=0,
        ),
    )(here, cotangent.reshape(2 * tokens, width), param_shard.reshape(2 * rows, width), activations)


def other_kernel(groups, here, cot, activations, up_one, down_one, *refs):
    outs, held, sems = refs[:-2], refs[-2], refs[-1]
    fetch_all(groups, here, activations, held, sems)
    multiply_all(groups, here, cot, activations, outs, held, sems, (up_one, down_one))


def other_terms(here, groups, cot_t, activations, up_one, down_one, rows):
    total = sum(count for _, _, count in groups)
    columns, tokens = cot_t.shape
    in_vmem = pl.BlockSpec(memory_space=pltpu.VMEM)
    return pl.pallas_call(
        functools.partial(other_kernel, groups),
        out_shape=[
            jax.ShapeDtypeStruct((4, 2, columns, rows), jnp.bfloat16) for _ in range(len(groups) // 2)
        ],
        in_specs=[
            pl.BlockSpec(memory_space=pltpu.SMEM),
            in_vmem,
            pl.BlockSpec(memory_space=pl.ANY),
            in_vmem,
            in_vmem,
        ],
        scratch_shapes=[
            pltpu.VMEM((total, tokens, 2 * rows), jnp.bfloat16),
            pltpu.SemaphoreType.DMA((total, 2)),
        ],
        compiler_params=MOST,
        cost_estimate=pl.CostEstimate(
            flops=4 * total * columns * tokens * rows,
            bytes_accessed=4 * total * rows * (tokens + columns) + 2 * columns * tokens,
            transcendentals=0,
        ),
    )(here, cot_t, activations, up_one, down_one)


def adam_kernel(mine, theirs, master_in, first_in, second_in, new_master, moments, layer):
    grad = (mine[...].astype(jnp.float32) + theirs[...].astype(jnp.float32)).T
    rows = grad.shape[0]
    width = grad.shape[1] // 2
    for j in range(2):
        at = pl.ds(j, rows, stride=2)
        weight_grad = grad[:, j * width : (j + 1) * width]
        master = master_in[at, :]
        first = beta_one * first_in[at, :] + (1.0 - beta_one) * weight_grad
        second = beta_two * second_in[at, :] + (1.0 - beta_two) * weight_grad * weight_grad
        first_hat = first / (1.0 - beta_one**step_number)
        second_hat = second / (1.0 - beta_two**step_number)
        new_master[at, :] = master - learn_rate * (
            first_hat / (jnp.sqrt(second_hat) + epsilon) + decay_rate * master
        )
        moments[0, j] = first.astype(jnp.bfloat16)
        moments[1, j] = second.astype(jnp.bfloat16)
    layer[...] = new_master[...].astype(jnp.bfloat16)


def adam(mine, theirs, master, first, second):
    rows, width = master.shape
    return pl.pallas_call(
        adam_kernel,
        out_shape=(
            jax.ShapeDtypeStruct((rows, width), jnp.float32),
            jax.ShapeDtypeStruct((2, 2, rows // 2, width), jnp.bfloat16),
            jax.ShapeDtypeStruct((rows, width), jnp.bfloat16),
        ),
        compiler_params=WIDE,
        cost_estimate=pl.CostEstimate(
            flops=20 * rows * width, bytes_accessed=30 * rows * width, transcendentals=2 * rows * width
        ),
    )(mine, theirs, master, first, second)


def place_kernel(groups, here, *refs):
    sources, out, sems = refs[: len(groups)], refs[-2], refs[-1]
    copies = []
    for source, (first, second) in zip(sources, groups):
        for i in range(source.shape[0]):
            for s in range(2):
                at = block_at(here, first, second + i, s, out.shape[0])
                copies.append(pltpu.make_async_copy(source.at[i, s], out.at[at], sems.at[len(copies)]))
    for copy in copies:
        copy.start()
    for copy in copies:
        copy.wait()


def place(here, groups, sources, total, into=None):
    block = sources[0].shape[2:]
    held = [] if into is None else [into]
    count = 2 * sum(source.shape[0] for source in sources)
    any_space = pl.BlockSpec(memory_space=pl.ANY)
    return pl.pallas_call(
        functools.partial(place_kernel, groups),
        out_shape=jax.ShapeDtypeStruct((total,) + block, sources[0].dtype),
        in_specs=[pl.BlockSpec(memory_space=pltpu.SMEM)]
        + [pl.BlockSpec(memory_space=pltpu.VMEM)] * len(sources)
        + [any_space] * len(held),
        out_specs=any_space,
        scratch_shapes=[pltpu.SemaphoreType.DMA((count,))],
        input_output_aliases={} if into is None else {1 + len(sources): 0},
        compiler_params=WIDE,
        cost_estimate=pl.CostEstimate(flops=0, bytes_accessed=0, transcendentals=0),
    )(here, *sources, *held)


def input_kernel(here, cot_mine, cot_theirs, params, out, total):
    step = pl.program_id(0)
    rows = params.shape[3]
    c = here[4]

    @pl.when(step == 0)
    def _():
        total[...] = jnp.zeros_like(total)

    for part in range(2):
        for s in range(2):
            at = slice((2 * part + s) * rows, (2 * part + s + 1) * rows)
            total[:, at] += jnp.dot(
                cot_mine[0], params[2 * c + part, s], preferred_element_type=jnp.float32
            ) + jnp.dot(cot_theirs[0], params[2 - 2 * c + part, s], preferred_element_type=jnp.float32)

    @pl.when(step == pl.num_programs(0) - 1)
    def _():
        out[...] = total[...].astype(out.dtype)


def input_matmul(here, cot_mine, cot_theirs, params):
    chips, tokens, columns = cot_mine.shape
    rows = params.shape[3]
    cot_spec = pl.BlockSpec((1, tokens, columns), lambda k, here: (k, 0, 0))
    return pl.pallas_call(
        input_kernel,
        out_shape=jax.ShapeDtypeStruct((tokens, 4 * rows), jnp.bfloat16),
        grid_spec=pltpu.PrefetchScalarGridSpec(
            num_scalar_prefetch=1,
            grid=(chips,),
            in_specs=[
                cot_spec,
                cot_spec,
                pl.BlockSpec((4, 2, columns, rows), lambda k, here: ((here[3] + 4 - k) % 4, 0, 0, 0)),
            ],
            out_specs=pl.BlockSpec((tokens, 4 * rows), lambda k, here: (0, 0)),
            scratch_shapes=[pltpu.VMEM((tokens, 4 * rows), jnp.float32)],
        ),
        compiler_params=MOST,
        cost_estimate=pl.CostEstimate(flops=0, bytes_accessed=0, transcendentals=0),
    )(here, cot_mine, cot_theirs, params)


def add(*terms):
    total = terms[0].astype(jnp.float32)
    for term in terms[1:]:
        total = total + term.astype(jnp.float32)
    return total.astype(jnp.bfloat16)


def tie(*values):
    return lax.optimization_barrier(values)


def per_device(activations, cotangent, param_shard, master_store, first_store, second_store):
    x, y, h, l, c = (lax.axis_index(a) for a in AXES)
    tokens, _, width = cotangent.shape
    rows = param_shard.shape[0]
    columns = 2 * width
    here = jnp.stack([x, y, h, l, c]).astype(jnp.int32)

    flat_cot, cot_t, par, up, down = first_terms(
        here, ((2, 0, 2), (2, 2, 2)), cotangent, param_shard, activations
    )
    up_one, down_one = move(up, along_first(1)), move(down, along_first(-1))
    par_same, par_other = move(par, to_user), move(par, to_user_across)
    cots = [flat_cot, move(flat_cot, next_in_line)]
    up, down, own = other_terms(
        here,
        ((1, 0, 2), (1, 2, 2), (3, 0, 2), (3, 2, 2), (0, 0, 2), (0, 2, 2)),
        cot_t,
        activations,
        up_one,
        down_one,
        rows,
    )
    up, down, par_same, par_other, cots[1] = tie(up, down, par_same, par_other, cots[1])
    up_two, down_two = move(up, along_first(1)), move(down, along_first(-1))
    pair = jnp.where(h == 0, jnp.stack([par_same, par_other]), jnp.stack([par_other, par_same]))
    params = lax.all_gather(pair, ("x", "y"), axis=0)
    cots += [move(cots[1], next_in_line), move(flat_cot, back_in_line)]
    sums = [add(own[i], up_two[i], down_two[i]) for i in range(4)]

    sums[1], sums[2], sums[3], cots[2], cots[3] = tie(*sums[1:], cots[2], cots[3])
    cot_mine = jnp.stack(cots)
    cot_theirs = move(cot_mine, other_core)
    got = [
        move(sums[1], along_second(1)),
        move(sums[3], along_second(-1)),
        move(sums[2], along_second(2)),
    ]
    far = add(sums[0][1], *(g[1] for g in got))
    near = add(sums[0][0], *(g[0] for g in got))
    far, cot_theirs = tie(far, cot_theirs)
    state = [v.reshape(2 * rows, width) for v in (master_store, first_store, second_store)]
    new_master, moments, layer = adam(near, move(far, other_half), *state)

    layer_other = move(layer, other_half)
    layer_other, moments = tie(layer_other, moments)
    moments = move(moments, previous_block)
    pair = jnp.where(h == 0, jnp.stack([layer, layer_other]), jnp.stack([layer_other, layer]))
    from_up = move(pair, along_second(-1))
    from_down = move(pair, along_second(1))
    from_far = move(pair, along_second(2))
    four = jnp.stack([pair, from_up, from_far, from_down])
    four, new_master = tie(four, new_master)
    four_down, four_up = move(four, along_first(1)), move(four, along_first(-1))
    new_master = move(new_master, previous_block)
    low, high, new_master = tie(four_down[:2], four_up[2:], new_master)
    low_far, high_far = move(low, along_first(1)), move(high, along_first(-1))
    input_grad = input_matmul(here, cot_mine, cot_theirs, params)
    new_layer = place(here, ((0, 0), (1, 0), (-1, 0)), [four, four_up, four_down], 32)
    new_layer, input_grad = tie(new_layer, input_grad)
    new_layer = place(here, ((2, 0), (2, 2)), [low_far, high_far], 32, new_layer)

    shape = (rows, 2, width)
    moments = moments.astype(jnp.float32).transpose(0, 2, 1, 3)
    return (
        input_grad,
        new_master.reshape(shape),
        moments[0],
        moments[1],
        new_layer.reshape(32 * rows, 2, width),
    )


def solution(mesh):
    fine = Mesh(mesh.devices.reshape(tuple(SIZES.values())), AXES)
    return jax.shard_map(
        per_device,
        mesh=fine,
        in_specs=(
            P(DP, None),
            P(DP, None, MP),
            P(DP, None, MP),
            P(DP, None, MP),
            P(DP, None, MP),
            P(DP, None, MP),
        ),
        out_specs=(
            P(DP, MP),
            P(DP, None, MP),
            P(DP, None, MP),
            P(DP, None, MP),
            P(None, None, MP),
        ),
        check_vma=False,
    )
```

```python
import functools

import jax
import jax.numpy as jnp
import numpy as np
from jax import lax
from jax.experimental import pallas as pl
from jax.experimental.pallas import tpu as pltpu
from jax.sharding import Mesh, PartitionSpec as P

learn_rate = 0.001
beta_one = 0.9
beta_two = 0.95
decay_rate = 0.1
epsilon = 1e-08
step_number = 10

SIZES = {"x": 4, "y": 4, "h": 2, "l": 4, "c": 2}
AXES = tuple(SIZES)
DP = ("x", "y", "h")
MP = ("l", "c")
MOST = pltpu.CompilerParams(vmem_limit_bytes=56 * 2**20)
WIDE = pltpu.CompilerParams(vmem_limit_bytes=32 * 2**20)


def move(value, target):
    shape = tuple(SIZES.values())
    pairs = []
    for source in range(int(np.prod(shape))):
        at = dict(zip(AXES, (int(i) for i in np.unravel_index(source, shape))))
        to = target(**at)
        pairs.append((source, int(np.ravel_multi_index([to[a] % SIZES[a] for a in AXES], shape))))
    return lax.ppermute(value, AXES, pairs)


def along_first(by):
    def target(x, y, h, l, c):
        return dict(x=x + by * (1 - c), y=y + by * c, h=h, l=l, c=c)

    return target


def along_second(by):
    def target(x, y, h, l, c):
        return dict(x=x + by * c, y=y + by * (1 - c), h=h, l=l, c=c)

    return target


def other_half(x, y, h, l, c):
    return dict(x=x, y=y, h=h + 1, l=l, c=c)


def other_core(x, y, h, l, c):
    return dict(x=x, y=y, h=h, l=l, c=c + 1)


def next_in_line(x, y, h, l, c):
    return dict(x=x, y=y, h=h, l=l + 1, c=c)


def back_in_line(x, y, h, l, c):
    return dict(x=x, y=y, h=h, l=l - 1, c=c)


def previous_block(x, y, h, l, c):
    block = (x * 8 + y * 2 + h - 1) % 32
    return dict(x=block // 8, y=block // 2 % 4, h=block % 2, l=l, c=c)


def to_user(x, y, h, l, c):
    return dict(x=l, y=2 * c + y % 2, h=h, l=x, c=y // 2)


def to_user_across(x, y, h, l, c):
    return dict(to_user(x, y, h, l, c), h=h + 1)


def pair_at(here, first, second):
    x, y, c = here[0], here[1], here[4]
    first, second = (x + c * (y - x) + first) % 4, (y + c * (x - y) + second) % 4
    return 4 * (first + c * (second - first)) + second + c * (first - second)


def block_at(here, first, second, s, blocks):
    return (2 * pair_at(here, first, second) + blocks - 1 + s) % blocks


def fetch(here, activations, held, sems, g, first, second, s):
    rows = held.shape[2] // 2
    block = block_at(here, first, second, s, activations.shape[1] // rows)
    return pltpu.make_async_copy(
        activations.at[:, pl.ds(pl.multiple_of(block * rows, rows), rows)],
        held.at[g, :, pl.ds(s * rows, rows)],
        sems.at[g, s],
    )


def fetch_all(groups, here, activations, held, sems):
    g = 0
    for first, second, count in groups:
        for i in range(count):
            for s in range(2):
                fetch(here, activations, held, sems, g, first, second + i, s).start()
            g += 1


def multiply_all(groups, here, cot, activations, outs, held, sems, received=()):
    rows = held.shape[2] // 2
    done = 0
    for n, (first, second, count) in enumerate(groups):
        out = outs[n // 2] if received else outs[n]
        base = 2 * (n % 2) if received else 0
        got = received[n // 2] if received and n in (0, 3) else None

        def step(i, carry, out=out, base=base, got=got, done=done, first=first, second=second):
            for s in range(2):
                fetch(here, activations, held, sems, done + i, first, second + i, s).wait()
            both = jnp.dot(cot[...], held[done + i], preferred_element_type=jnp.float32)
            for s in range(2):
                term = both[:, s * rows : (s + 1) * rows]
                if got is not None:
                    term += got[i, here[2] ^ s].astype(jnp.float32)
                out[base + i, here[2] ^ s] = term.astype(out.dtype)
            return carry

        lax.fori_loop(0, count, step, 0)
        done += count


def first_kernel(groups, here, cot_in, par_in, activations, *refs):
    cot, cot_t, par_t, *outs = refs[: 3 + len(groups)]
    held, sems, cot_raw, par_raw, raw_sems, wide = refs[3 + len(groups) :]
    raw = (
        pltpu.make_async_copy(cot_in, cot_raw, raw_sems.at[0]),
        pltpu.make_async_copy(par_in, par_raw, raw_sems.at[1]),
    )
    raw[0].start()
    fetch_all(groups, here, activations, held, sems)
    raw[1].start()
    for copy, source, plain, turned in ((raw[0], cot_raw, cot, cot_t), (raw[1], par_raw, None, par_t)):
        copy.wait()
        rows, width = source.shape[0] // 2, source.shape[1]
        wide[: 2 * rows, :] = source[...].astype(jnp.float32)
        for j in range(2):
            part = wide[pl.ds(j, rows, stride=2), :]
            at = slice(j * width, (j + 1) * width)
            if plain is not None:
                plain[:, at] = part.astype(plain.dtype)
            turned[at, :] = part.T.astype(turned.dtype)
    multiply_all(groups, here, cot_t, activations, outs, held, sems)


def first_terms(here, groups, cotangent, param_shard, activations):
    tokens, rows = cotangent.shape[0], param_shard.shape[0]
    width = cotangent.shape[2]
    total = sum(count for _, _, count in groups)
    any_space = pl.BlockSpec(memory_space=pl.ANY)
    shapes = [(tokens, 2 * width), (2 * width, tokens), (2 * width, rows)]
    shapes += [(count, 2, 2 * width, rows) for _, _, count in groups]
    return pl.pallas_call(
        functools.partial(first_kernel, groups),
        out_shape=[jax.ShapeDtypeStruct(shape, jnp.bfloat16) for shape in shapes],
        in_specs=[pl.BlockSpec(memory_space=pltpu.SMEM), any_space, any_space, any_space],
        scratch_shapes=[
            pltpu.VMEM((total, tokens, 2 * rows), jnp.bfloat16),
            pltpu.SemaphoreType.DMA((total, 2)),
            pltpu.VMEM((2 * tokens, width), jnp.bfloat16),
            pltpu.VMEM((2 * rows, width), jnp.bfloat16),
            pltpu.SemaphoreType.DMA((2,)),
            pltpu.VMEM((2 * max(tokens, rows), width), jnp.float32),
        ],
        compiler_params=MOST,
        cost_estimate=pl.CostEstimate(
            flops=8 * total * width * tokens * rows,
            bytes_accessed=4 * total * rows * (tokens + 2 * width) + 12 * width * tokens,
            transcendentals=0,
        ),
    )(here, cotangent.reshape(2 * tokens, width), param_shard.reshape(2 * rows, width), activations)


def other_kernel(groups, here, cot, activations, up_one, down_one, *refs):
    outs, held, sems = refs[:-2], refs[-2], refs[-1]
    fetch_all(groups, here, activations, held, sems)
    multiply_all(groups, here, cot, activations, outs, held, sems, (up_one, down_one))


def other_terms(here, groups, cot_t, activations, up_one, down_one, rows):
    total = sum(count for _, _, count in groups)
    columns, tokens = cot_t.shape
    in_vmem = pl.BlockSpec(memory_space=pltpu.VMEM)
    return pl.pallas_call(
        functools.partial(other_kernel, groups),
        out_shape=[
            jax.ShapeDtypeStruct((4, 2, columns, rows), jnp.bfloat16) for _ in range(len(groups) // 2)
        ],
        in_specs=[
            pl.BlockSpec(memory_space=pltpu.SMEM),
            in_vmem,
            pl.BlockSpec(memory_space=pl.ANY),
            in_vmem,
            in_vmem,
        ],
        scratch_shapes=[
            pltpu.VMEM((total, tokens, 2 * rows), jnp.bfloat16),
            pltpu.SemaphoreType.DMA((total, 2)),
        ],
        compiler_params=MOST,
        cost_estimate=pl.CostEstimate(
            flops=4 * total * columns * tokens * rows,
            bytes_accessed=4 * total * rows * (tokens + columns) + 2 * columns * tokens,
            transcendentals=0,
        ),
    )(here, cot_t, activations, up_one, down_one)


def adam_kernel(mine, theirs, master_in, first_in, second_in, new_master, new_first, new_second, layer):
    grad = (mine[...].astype(jnp.float32) + theirs[...].astype(jnp.float32)).T
    rows = grad.shape[0]
    width = grad.shape[1] // 2
    for j in range(2):
        at = pl.ds(j, rows, stride=2)
        weight_grad = grad[:, j * width : (j + 1) * width]
        master = master_in[at, :]
        first = beta_one * first_in[at, :] + (1.0 - beta_one) * weight_grad
        second = beta_two * second_in[at, :] + (1.0 - beta_two) * weight_grad * weight_grad
        first_hat = first / (1.0 - beta_one**step_number)
        second_hat = second / (1.0 - beta_two**step_number)
        new_master[at, :] = master - learn_rate * (
            first_hat / (jnp.sqrt(second_hat) + epsilon) + decay_rate * master
        )
        new_first[j] = first.astype(jnp.bfloat16)
        new_second[j] = second.astype(jnp.bfloat16)
    layer[...] = new_master[...].astype(jnp.bfloat16)


def adam(mine, theirs, master, first, second):
    rows, width = master.shape
    return pl.pallas_call(
        adam_kernel,
        out_shape=(
            jax.ShapeDtypeStruct((rows, width), jnp.float32),
            *[jax.ShapeDtypeStruct((2, rows // 2, width), jnp.bfloat16)] * 2,
            jax.ShapeDtypeStruct((rows, width), jnp.bfloat16),
        ),
        compiler_params=WIDE,
        cost_estimate=pl.CostEstimate(
            flops=20 * rows * width, bytes_accessed=30 * rows * width, transcendentals=2 * rows * width
        ),
    )(mine, theirs, master, first, second)


def copies_of(groups, here, sources, out, sems):
    copies = []
    for source, (first, second) in zip(sources, groups):
        for i in range(source.shape[0]):
            for s in range(2):
                at = block_at(here, first, second + i, s, out.shape[0])
                copies.append(pltpu.make_async_copy(source.at[i, s], out.at[at], sems.at[len(copies)]))
    return copies


def place_kernel(groups, here, *refs):
    copies = copies_of(groups, here, refs[: len(groups)], refs[-2], refs[-1])
    for copy in copies:
        copy.start()
    for copy in copies:
        copy.wait()


def place(here, groups, sources, total):
    block = sources[0].shape[2:]
    count = 2 * sum(source.shape[0] for source in sources)
    return pl.pallas_call(
        functools.partial(place_kernel, groups),
        out_shape=jax.ShapeDtypeStruct((total,) + block, sources[0].dtype),
        in_specs=[pl.BlockSpec(memory_space=pltpu.SMEM)]
        + [pl.BlockSpec(memory_space=pltpu.VMEM)] * len(sources),
        out_specs=pl.BlockSpec(memory_space=pl.ANY),
        scratch_shapes=[pltpu.SemaphoreType.DMA((count,))],
        compiler_params=WIDE,
        cost_estimate=pl.CostEstimate(flops=0, bytes_accessed=0, transcendentals=0),
    )(here, *sources)


def finish_kernel(groups, here, low, high, master_in, first_in, second_in, held, *refs):
    layer, master, first, second, sems = refs
    copies = copies_of(groups, here, (low, high), layer, sems)
    for copy in copies:
        copy.start()
    rows = first_in.shape[1]
    master[...] = master_in[...]
    for j in range(2):
        at = pl.ds(j, rows, stride=2)
        first[at, :] = first_in[j].astype(jnp.float32)
        second[at, :] = second_in[j].astype(jnp.float32)
    for copy in copies:
        copy.wait()


def finish(here, groups, low, high, master, first, second, layer):
    any_space = pl.BlockSpec(memory_space=pl.ANY)
    in_vmem = pl.BlockSpec(memory_space=pltpu.VMEM)
    state = jax.ShapeDtypeStruct(master.shape, jnp.float32)
    return pl.pallas_call(
        functools.partial(finish_kernel, groups),
        out_shape=[jax.ShapeDtypeStruct(layer.shape, layer.dtype), state, state, state],
        in_specs=[pl.BlockSpec(memory_space=pltpu.SMEM)] + [in_vmem] * 5 + [any_space],
        out_specs=[any_space] + [in_vmem] * 3,
        scratch_shapes=[pltpu.SemaphoreType.DMA((2 * (low.shape[0] + high.shape[0]),))],
        input_output_aliases={6: 0},
        compiler_params=WIDE,
        cost_estimate=pl.CostEstimate(flops=0, bytes_accessed=0, transcendentals=0),
    )(here, low, high, master, first, second, layer)


def input_kernel(here, cot_mine, cot_theirs, params, out, total):
    step = pl.program_id(0)
    rows = params.shape[3]
    c = here[4]

    @pl.when(step == 0)
    def _():
        total[...] = jnp.zeros_like(total)

    for part in range(2):
        for s in range(2):
            at = slice((2 * part + s) * rows, (2 * part + s + 1) * rows)
            total[:, at] += jnp.dot(
                cot_mine[0], params[2 * c + part, s], preferred_element_type=jnp.float32
            ) + jnp.dot(cot_theirs[0], params[2 - 2 * c + part, s], preferred_element_type=jnp.float32)

    @pl.when(step == pl.num_programs(0) - 1)
    def _():
        out[...] = total[...].astype(out.dtype)


def input_matmul(here, cot_mine, cot_theirs, params):
    chips, tokens, columns = cot_mine.shape
    rows = params.shape[3]
    cot_spec = pl.BlockSpec((1, tokens, columns), lambda k, here: (k, 0, 0))
    return pl.pallas_call(
        input_kernel,
        out_shape=jax.ShapeDtypeStruct((tokens, 4 * rows), jnp.bfloat16),
        grid_spec=pltpu.PrefetchScalarGridSpec(
            num_scalar_prefetch=1,
            grid=(chips,),
            in_specs=[
                cot_spec,
                cot_spec,
                pl.BlockSpec((4, 2, columns, rows), lambda k, here: ((here[3] + 4 - k) % 4, 0, 0, 0)),
            ],
            out_specs=pl.BlockSpec((tokens, 4 * rows), lambda k, here: (0, 0)),
            scratch_shapes=[pltpu.VMEM((tokens, 4 * rows), jnp.float32)],
        ),
        compiler_params=MOST,
        cost_estimate=pl.CostEstimate(
            flops=16 * chips * tokens * columns * rows,
            bytes_accessed=4 * chips * columns * (tokens + 2 * rows) + 8 * tokens * rows,
            transcendentals=0,
        ),
    )(here, cot_mine, cot_theirs, params)


def add(*terms):
    total = terms[0].astype(jnp.float32)
    for term in terms[1:]:
        total = total + term.astype(jnp.float32)
    return total.astype(jnp.bfloat16)


def tie(*values):
    return lax.optimization_barrier(values)


def per_device(activations, cotangent, param_shard, master_store, first_store, second_store):
    x, y, h, l, c = (lax.axis_index(a) for a in AXES)
    tokens, _, width = cotangent.shape
    rows = param_shard.shape[0]
    columns = 2 * width
    here = jnp.stack([x, y, h, l, c]).astype(jnp.int32)

    flat_cot, cot_t, par, up, down = first_terms(
        here, ((2, 0, 2), (2, 2, 2)), cotangent, param_shard, activations
    )
    up_one, down_one = move(up, along_first(1)), move(down, along_first(-1))
    par_same, par_other = move(par, to_user), move(par, to_user_across)
    cots = [flat_cot, move(flat_cot, next_in_line)]
    up, down, own = other_terms(
        here,
        ((1, 0, 2), (1, 2, 2), (3, 0, 2), (3, 2, 2), (0, 0, 2), (0, 2, 2)),
        cot_t,
        activations,
        up_one,
        down_one,
        rows,
    )
    up, down, par_same, par_other, cots[1] = tie(up, down, par_same, par_other, cots[1])
    up_two, down_two = move(up, along_first(1)), move(down, along_first(-1))
    pair = jnp.where(h == 0, jnp.stack([par_same, par_other]), jnp.stack([par_other, par_same]))
    params = lax.all_gather(pair, ("x", "y"), axis=0)
    cots += [move(cots[1], next_in_line), move(flat_cot, back_in_line)]
    sums = [add(own[i], up_two[i], down_two[i]) for i in range(4)]

    sums[1], sums[2], sums[3], cots[2], cots[3] = tie(*sums[1:], cots[2], cots[3])
    cot_mine = jnp.stack(cots)
    cot_theirs = move(cot_mine, other_core)
    got = [
        move(sums[1], along_second(1)),
        move(sums[3], along_second(-1)),
        move(sums[2], along_second(2)),
    ]
    far = add(sums[0][1], *(g[1] for g in got))
    near = add(sums[0][0], *(g[0] for g in got))
    far, cot_theirs = tie(far, cot_theirs)
    state = [v.reshape(2 * rows, width) for v in (master_store, first_store, second_store)]
    new_master, new_first, new_second, layer = adam(near, move(far, other_half), *state)

    layer_other = move(layer, other_half)
    layer_other, new_first = tie(layer_other, new_first)
    new_first = move(new_first, previous_block)
    pair = jnp.where(h == 0, jnp.stack([layer, layer_other]), jnp.stack([layer_other, layer]))
    from_up = move(pair, along_second(-1))
    from_down = move(pair, along_second(1))
    from_far = move(pair, along_second(2))
    four = jnp.stack([pair, from_up, from_far, from_down])
    four, new_master, new_first = tie(four, new_master, new_first)
    four_down, four_up = move(four, along_first(1)), move(four, along_first(-1))
    new_master = move(new_master, previous_block)
    input_grad = input_matmul(here, cot_mine, cot_theirs, params)
    four_down, four_up, input_grad, new_master, new_second = tie(
        four_down, four_up, input_grad, new_master, new_second
    )
    new_second = move(new_second, previous_block)
    low_far, high_far = move(four_down[:2], along_first(1)), move(four_up[2:], along_first(-1))
    new_layer = place(here, ((0, 0), (1, 0), (-1, 0)), [four, four_up, four_down], 32)
    new_layer, *state = finish(
        here, ((2, 0), (2, 2)), low_far, high_far, new_master, new_first, new_second, new_layer
    )
    new_master, new_first, new_second = (v.reshape(rows, 2, width) for v in state)
    return (
        input_grad,
        new_master,
        new_first,
        new_second,
        new_layer.reshape(32 * rows, 2, width),
    )


def solution(mesh):
    fine = Mesh(mesh.devices.reshape(tuple(SIZES.values())), AXES)
    return jax.shard_map(
        per_device,
        mesh=fine,
        in_specs=(
            P(DP, None),
            P(DP, None, MP),
            P(DP, None, MP),
            P(DP, None, MP),
            P(DP, None, MP),
            P(DP, None, MP),
        ),
        out_specs=(
            P(DP, MP),
            P(DP, None, MP),
            P(DP, None, MP),
            P(DP, None, MP),
            P(None, None, MP),
        ),
        check_vma=False,
    )
```

```python
import functools

import jax
import jax.numpy as jnp
import numpy as np
from jax import lax
from jax.experimental import pallas as pl
from jax.experimental.pallas import tpu as pltpu
from jax.sharding import Mesh, PartitionSpec as P

learn_rate = 0.001
beta_one = 0.9
beta_two = 0.95
decay_rate = 0.1
epsilon = 1e-08
step_number = 10

SIZES = {"x": 4, "y": 4, "h": 2, "l": 4, "c": 2}
AXES = tuple(SIZES)
DP = ("x", "y", "h")
MP = ("l", "c")
MOST = pltpu.CompilerParams(vmem_limit_bytes=56 * 2**20)
WIDE = pltpu.CompilerParams(vmem_limit_bytes=32 * 2**20)


def move(value, target):
    shape = tuple(SIZES.values())
    pairs = []
    for source in range(int(np.prod(shape))):
        at = dict(zip(AXES, (int(i) for i in np.unravel_index(source, shape))))
        to = target(**at)
        pairs.append((source, int(np.ravel_multi_index([to[a] % SIZES[a] for a in AXES], shape))))
    return lax.ppermute(value, AXES, pairs)


def along_first(by):
    def target(x, y, h, l, c):
        return dict(x=x + by * (1 - c), y=y + by * c, h=h, l=l, c=c)

    return target


def along_second(by):
    def target(x, y, h, l, c):
        return dict(x=x + by * c, y=y + by * (1 - c), h=h, l=l, c=c)

    return target


def other_half(x, y, h, l, c):
    return dict(x=x, y=y, h=h + 1, l=l, c=c)


def other_core(x, y, h, l, c):
    return dict(x=x, y=y, h=h, l=l, c=c + 1)


def next_in_line(x, y, h, l, c):
    return dict(x=x, y=y, h=h, l=l + 1, c=c)


def back_in_line(x, y, h, l, c):
    return dict(x=x, y=y, h=h, l=l - 1, c=c)


def previous_block(x, y, h, l, c):
    block = (x * 8 + y * 2 + h - 1) % 32
    return dict(x=block // 8, y=block // 2 % 4, h=block % 2, l=l, c=c)


def to_user(x, y, h, l, c):
    return dict(x=l, y=2 * c + y % 2, h=h, l=x, c=y // 2)


def to_user_across(x, y, h, l, c):
    return dict(to_user(x, y, h, l, c), h=h + 1)


def pair_at(here, first, second):
    x, y, c = here[0], here[1], here[4]
    first, second = (x + c * (y - x) + first) % 4, (y + c * (x - y) + second) % 4
    return 4 * (first + c * (second - first)) + second + c * (first - second)


def block_at(here, first, second, s, blocks):
    return (2 * pair_at(here, first, second) + blocks - 1 + s) % blocks


def fetch(here, activations, held, sems, g, first, second, s):
    rows = held.shape[2] // 2
    block = block_at(here, first, second, s, activations.shape[1] // rows)
    return pltpu.make_async_copy(
        activations.at[:, pl.ds(pl.multiple_of(block * rows, rows), rows)],
        held.at[g, :, pl.ds(s * rows, rows)],
        sems.at[g, s],
    )


def fetch_all(groups, here, activations, held, sems):
    g = 0
    for first, second, count in groups:
        for i in range(count):
            for s in range(2):
                fetch(here, activations, held, sems, g, first, second + i, s).start()
            g += 1


def multiply_all(groups, here, cot, activations, outs, held, sems, received=()):
    rows = held.shape[2] // 2
    done = 0
    for n, (first, second, count) in enumerate(groups):
        out = outs[n // 2] if received else outs[n]
        base = 2 * (n % 2) if received else 0
        got = received[n // 2] if received and n in (0, 3) else None

        def step(i, carry, out=out, base=base, got=got, done=done, first=first, second=second):
            for s in range(2):
                fetch(here, activations, held, sems, done + i, first, second + i, s).wait()
            both = jnp.dot(cot[...], held[done + i], preferred_element_type=jnp.float32)
            for s in range(2):
                term = both[:, s * rows : (s + 1) * rows]
                if got is not None:
                    term += got[i, here[2] ^ s].astype(jnp.float32)
                out[base + i, here[2] ^ s] = term.astype(out.dtype)
            return carry

        lax.fori_loop(0, count, step, 0)
        done += count


def first_kernel(groups, here, cot_in, par_in, activations, *refs):
    cot, cot_t, par_t, *outs = refs[: 3 + len(groups)]
    held, sems, cot_raw, par_raw, raw_sems, wide = refs[3 + len(groups) :]
    raw = (
        pltpu.make_async_copy(cot_in, cot_raw, raw_sems.at[0]),
        pltpu.make_async_copy(par_in, par_raw, raw_sems.at[1]),
    )
    raw[0].start()
    fetch_all(groups, here, activations, held, sems)
    raw[1].start()
    for copy, source, plain, turned in ((raw[0], cot_raw, cot, cot_t), (raw[1], par_raw, None, par_t)):
        copy.wait()
        rows, width = source.shape[0] // 2, source.shape[1]
        wide[: 2 * rows, :] = source[...].astype(jnp.float32)
        for j in range(2):
            part = wide[pl.ds(j, rows, stride=2), :]
            at = slice(j * width, (j + 1) * width)
            if plain is not None:
                plain[:, at] = part.astype(plain.dtype)
            turned[at, :] = part.T.astype(turned.dtype)
    multiply_all(groups, here, cot_t, activations, outs, held, sems)


def first_terms(here, groups, cotangent, param_shard, activations):
    tokens, rows = cotangent.shape[0], param_shard.shape[0]
    width = cotangent.shape[2]
    total = sum(count for _, _, count in groups)
    any_space = pl.BlockSpec(memory_space=pl.ANY)
    shapes = [(tokens, 2 * width), (2 * width, tokens), (2 * width, rows)]
    shapes += [(count, 2, 2 * width, rows) for _, _, count in groups]
    return pl.pallas_call(
        functools.partial(first_kernel, groups),
        out_shape=[jax.ShapeDtypeStruct(shape, jnp.bfloat16) for shape in shapes],
        in_specs=[pl.BlockSpec(memory_space=pltpu.SMEM), any_space, any_space, any_space],
        scratch_shapes=[
            pltpu.VMEM((total, tokens, 2 * rows), jnp.bfloat16),
            pltpu.SemaphoreType.DMA((total, 2)),
            pltpu.VMEM((2 * tokens, width), jnp.bfloat16),
            pltpu.VMEM((2 * rows, width), jnp.bfloat16),
            pltpu.SemaphoreType.DMA((2,)),
            pltpu.VMEM((2 * max(tokens, rows), width), jnp.float32),
        ],
        compiler_params=MOST,
        cost_estimate=pl.CostEstimate(
            flops=8 * total * width * tokens * rows,
            bytes_accessed=4 * total * rows * (tokens + 2 * width) + 12 * width * tokens,
            transcendentals=0,
        ),
    )(here, cotangent.reshape(2 * tokens, width), param_shard.reshape(2 * rows, width), activations)


def other_kernel(groups, here, cot, activations, up_one, down_one, *refs):
    outs, held, sems = refs[:-2], refs[-2], refs[-1]
    fetch_all(groups, here, activations, held, sems)
    multiply_all(groups, here, cot, activations, outs, held, sems, (up_one, down_one))


def other_terms(here, groups, cot_t, activations, up_one, down_one, rows):
    total = sum(count for _, _, count in groups)
    columns, tokens = cot_t.shape
    in_vmem = pl.BlockSpec(memory_space=pltpu.VMEM)
    return pl.pallas_call(
        functools.partial(other_kernel, groups),
        out_shape=[
            jax.ShapeDtypeStruct((4, 2, columns, rows), jnp.bfloat16) for _ in range(len(groups) // 2)
        ],
        in_specs=[
            pl.BlockSpec(memory_space=pltpu.SMEM),
            in_vmem,
            pl.BlockSpec(memory_space=pl.ANY),
            in_vmem,
            in_vmem,
        ],
        scratch_shapes=[
            pltpu.VMEM((total, tokens, 2 * rows), jnp.bfloat16),
            pltpu.SemaphoreType.DMA((total, 2)),
        ],
        compiler_params=MOST,
        cost_estimate=pl.CostEstimate(
            flops=4 * total * columns * tokens * rows,
            bytes_accessed=4 * total * rows * (tokens + columns) + 2 * columns * tokens,
            transcendentals=0,
        ),
    )(here, cot_t, activations, up_one, down_one)


def adam_kernel(mine, theirs, master_in, first_in, second_in, sent, layer, new_master):
    grad = (mine[...].astype(jnp.float32) + theirs[...].astype(jnp.float32)).T
    rows = grad.shape[0]
    width = grad.shape[1] // 2
    for j in range(2):
        at = pl.ds(j, rows, stride=2)
        weight_grad = grad[:, j * width : (j + 1) * width]
        master = master_in[at, :]
        first = beta_one * first_in[at, :] + (1.0 - beta_one) * weight_grad
        second = beta_two * second_in[at, :] + (1.0 - beta_two) * weight_grad * weight_grad
        first_hat = first / (1.0 - beta_one**step_number)
        second_hat = second / (1.0 - beta_two**step_number)
        new_master[at, :] = master = master - learn_rate * (
            first_hat / (jnp.sqrt(second_hat) + epsilon) + decay_rate * master
        )
        sent[0, j] = first.astype(jnp.bfloat16)
        sent[1, j] = second.astype(jnp.bfloat16)
        sent[2, j] = master.astype(jnp.bfloat16)
        sent[3, j] = (master - sent[2, j].astype(jnp.float32)).astype(jnp.bfloat16)
    layer[...] = new_master[...].astype(jnp.bfloat16)


def adam(mine, theirs, master, first, second):
    rows, width = master.shape
    return pl.pallas_call(
        adam_kernel,
        out_shape=(
            jax.ShapeDtypeStruct((4, 2, rows // 2, width), jnp.bfloat16),
            jax.ShapeDtypeStruct((rows, width), jnp.bfloat16),
        ),
        scratch_shapes=[pltpu.VMEM((rows, width), jnp.float32)],
        compiler_params=WIDE,
        cost_estimate=pl.CostEstimate(
            flops=20 * rows * width, bytes_accessed=30 * rows * width, transcendentals=2 * rows * width
        ),
    )(mine, theirs, master, first, second)


def place_kernel(groups, here, *refs):
    sources, out, sems = refs[: len(groups)], refs[-2], refs[-1]
    copies = []
    for source, (first, second) in zip(sources, groups):
        for i in range(source.shape[0]):
            for s in range(2):
                at = block_at(here, first, second + i, s, out.shape[0])
                copies.append(pltpu.make_async_copy(source.at[i, s], out.at[at], sems.at[len(copies)]))
    for copy in copies:
        copy.start()
    for copy in copies:
        copy.wait()


def place(here, groups, sources, total, into=None):
    block = sources[0].shape[2:]
    held = [] if into is None else [into]
    count = 2 * sum(source.shape[0] for source in sources)
    any_space = pl.BlockSpec(memory_space=pl.ANY)
    return pl.pallas_call(
        functools.partial(place_kernel, groups),
        out_shape=jax.ShapeDtypeStruct((total,) + block, sources[0].dtype),
        in_specs=[pl.BlockSpec(memory_space=pltpu.SMEM)]
        + [pl.BlockSpec(memory_space=pltpu.VMEM)] * len(sources)
        + [any_space] * len(held),
        out_specs=any_space,
        scratch_shapes=[pltpu.SemaphoreType.DMA((count,))],
        input_output_aliases={} if into is None else {1 + len(sources): 0},
        compiler_params=WIDE,
        cost_estimate=pl.CostEstimate(flops=0, bytes_accessed=0, transcendentals=0),
    )(here, *sources, *held)


def unpack_kernel(sent, master, first, second):
    rows = sent.shape[2]
    for j in range(2):
        at = pl.ds(j, rows, stride=2)
        first[at, :] = sent[0, j].astype(jnp.float32)
        second[at, :] = sent[1, j].astype(jnp.float32)
        master[at, :] = sent[2, j].astype(jnp.float32) + sent[3, j].astype(jnp.float32)


def unpack(sent):
    _, _, rows, width = sent.shape
    return pl.pallas_call(
        unpack_kernel,
        out_shape=[jax.ShapeDtypeStruct((2 * rows, width), jnp.float32)] * 3,
        compiler_params=WIDE,
        cost_estimate=pl.CostEstimate(flops=0, bytes_accessed=10 * sent.size, transcendentals=0),
    )(sent)


def input_kernel(here, cot_mine, cot_theirs, params, out, total):
    step = pl.program_id(0)
    rows = params.shape[3]
    c = here[4]

    @pl.when(step == 0)
    def _():
        total[...] = jnp.zeros_like(total)

    for part in range(2):
        for s in range(2):
            at = slice((2 * part + s) * rows, (2 * part + s + 1) * rows)
            total[:, at] += jnp.dot(
                cot_mine[0], params[2 * c + part, s], preferred_element_type=jnp.float32
            ) + jnp.dot(cot_theirs[0], params[2 - 2 * c + part, s], preferred_element_type=jnp.float32)

    @pl.when(step == pl.num_programs(0) - 1)
    def _():
        out[...] = total[...].astype(out.dtype)


def input_matmul(here, cot_mine, cot_theirs, params):
    chips, tokens, columns = cot_mine.shape
    rows = params.shape[3]
    cot_spec = pl.BlockSpec((1, tokens, columns), lambda k, here: (k, 0, 0))
    return pl.pallas_call(
        input_kernel,
        out_shape=jax.ShapeDtypeStruct((tokens, 4 * rows), jnp.bfloat16),
        grid_spec=pltpu.PrefetchScalarGridSpec(
            num_scalar_prefetch=1,
            grid=(chips,),
            in_specs=[
                cot_spec,
                cot_spec,
                pl.BlockSpec((4, 2, columns, rows), lambda k, here: ((here[3] + 4 - k) % 4, 0, 0, 0)),
            ],
            out_specs=pl.BlockSpec((tokens, 4 * rows), lambda k, here: (0, 0)),
            scratch_shapes=[pltpu.VMEM((tokens, 4 * rows), jnp.float32)],
        ),
        compiler_params=MOST,
        cost_estimate=pl.CostEstimate(
            flops=16 * chips * tokens * columns * rows,
            bytes_accessed=4 * chips * columns * (tokens + 2 * rows) + 8 * tokens * rows,
            transcendentals=0,
        ),
    )(here, cot_mine, cot_theirs, params)


def add(*terms):
    total = terms[0].astype(jnp.float32)
    for term in terms[1:]:
        total = total + term.astype(jnp.float32)
    return total.astype(jnp.bfloat16)


def tie(*values):
    return lax.optimization_barrier(values)


def per_device(activations, cotangent, param_shard, master_store, first_store, second_store):
    x, y, h, l, c = (lax.axis_index(a) for a in AXES)
    tokens, _, width = cotangent.shape
    rows = param_shard.shape[0]
    columns = 2 * width
    here = jnp.stack([x, y, h, l, c]).astype(jnp.int32)

    flat_cot, cot_t, par, up, down = first_terms(
        here, ((2, 0, 2), (2, 2, 2)), cotangent, param_shard, activations
    )
    up_one, down_one = move(up, along_first(1)), move(down, along_first(-1))
    par_same, par_other = move(par, to_user), move(par, to_user_across)
    cots = [flat_cot, move(flat_cot, next_in_line)]
    up, down, own = other_terms(
        here,
        ((1, 0, 2), (1, 2, 2), (3, 0, 2), (3, 2, 2), (0, 0, 2), (0, 2, 2)),
        cot_t,
        activations,
        up_one,
        down_one,
        rows,
    )
    up, down, par_same, par_other, cots[1] = tie(up, down, par_same, par_other, cots[1])
    up_two, down_two = move(up, along_first(1)), move(down, along_first(-1))
    pair = jnp.where(h == 0, jnp.stack([par_same, par_other]), jnp.stack([par_other, par_same]))
    params = lax.all_gather(pair, ("x", "y"), axis=0)
    cots += [move(cots[1], next_in_line), move(flat_cot, back_in_line)]
    sums = [add(own[i], up_two[i], down_two[i]) for i in range(4)]

    sums[1], sums[2], sums[3], cots[2], cots[3] = tie(*sums[1:], cots[2], cots[3])
    cot_mine = jnp.stack(cots)
    cot_theirs = move(cot_mine, other_core)
    got = [
        move(sums[1], along_second(1)),
        move(sums[3], along_second(-1)),
        move(sums[2], along_second(2)),
    ]
    far = add(sums[0][1], *(g[1] for g in got))
    near = add(sums[0][0], *(g[0] for g in got))
    far, cot_theirs = tie(far, cot_theirs)
    state = [v.reshape(2 * rows, width) for v in (master_store, first_store, second_store)]
    sent, layer = adam(near, move(far, other_half), *state)

    layer_other = move(layer, other_half)
    pair = jnp.where(h == 0, jnp.stack([layer, layer_other]), jnp.stack([layer_other, layer]))
    from_up = move(pair, along_second(-1))
    from_down = move(pair, along_second(1))
    from_far = move(pair, along_second(2))
    four = jnp.stack([pair, from_up, from_far, from_down])
    four, sent = tie(four, sent)
    four_down, four_up = move(four, along_first(1)), move(four, along_first(-1))
    sent = move(sent, previous_block)
    input_grad = input_matmul(here, cot_mine, cot_theirs, params)
    four_down, four_up, input_grad = tie(four_down, four_up, input_grad)
    low_far, high_far = move(four_down[:2], along_first(1)), move(four_up[2:], along_first(-1))
    new_layer = place(here, ((0, 0), (1, 0), (-1, 0)), [four, four_up, four_down], 32)
    new_layer, sent = tie(new_layer, sent)
    new_layer, *state = tie(new_layer, *unpack(sent))
    new_layer = place(here, ((2, 0), (2, 2)), [low_far, high_far], 32, new_layer)
    new_master, new_first, new_second = (v.reshape(rows, 2, width) for v in state)
    return (
        input_grad,
        new_master,
        new_first,
        new_second,
        new_layer.reshape(32 * rows, 2, width),
    )


def solution(mesh):
    fine = Mesh(mesh.devices.reshape(tuple(SIZES.values())), AXES)
    return jax.shard_map(
        per_device,
        mesh=fine,
        in_specs=(
            P(DP, None),
            P(DP, None, MP),
            P(DP, None, MP),
            P(DP, None, MP),
            P(DP, None, MP),
            P(DP, None, MP),
        ),
        out_specs=(
            P(DP, MP),
            P(DP, None, MP),
            P(DP, None, MP),
            P(DP, None, MP),
            P(None, None, MP),
        ),
        check_vma=False,
    )
```

```python
import functools

import jax
import jax.numpy as jnp
import numpy as np
from jax import lax
from jax.experimental import pallas as pl
from jax.experimental.pallas import tpu as pltpu
from jax.sharding import Mesh, PartitionSpec as P

learn_rate = 0.001
beta_one = 0.9
beta_two = 0.95
decay_rate = 0.1
epsilon = 1e-08
step_number = 10

SIZES = {"x": 4, "y": 4, "h": 2, "l": 4, "c": 2}
AXES = tuple(SIZES)
DP = ("x", "y", "h")
MP = ("l", "c")
MOST = pltpu.CompilerParams(vmem_limit_bytes=56 * 2**20)
WIDE = pltpu.CompilerParams(vmem_limit_bytes=32 * 2**20)


def move(value, target):
    shape = tuple(SIZES.values())
    pairs = []
    for source in range(int(np.prod(shape))):
        at = dict(zip(AXES, (int(i) for i in np.unravel_index(source, shape))))
        to = target(**at)
        pairs.append((source, int(np.ravel_multi_index([to[a] % SIZES[a] for a in AXES], shape))))
    return lax.ppermute(value, AXES, pairs)


def along_first(by):
    def target(x, y, h, l, c):
        return dict(x=x + by * (1 - c), y=y + by * c, h=h, l=l, c=c)

    return target


def along_second(by):
    def target(x, y, h, l, c):
        return dict(x=x + by * c, y=y + by * (1 - c), h=h, l=l, c=c)

    return target


def other_half(x, y, h, l, c):
    return dict(x=x, y=y, h=h + 1, l=l, c=c)


def other_core(x, y, h, l, c):
    return dict(x=x, y=y, h=h, l=l, c=c + 1)


def next_in_line(x, y, h, l, c):
    return dict(x=x, y=y, h=h, l=l + 1, c=c)


def back_in_line(x, y, h, l, c):
    return dict(x=x, y=y, h=h, l=l - 1, c=c)


def previous_block(x, y, h, l, c):
    block = (x * 8 + y * 2 + h - 1) % 32
    return dict(x=block // 8, y=block // 2 % 4, h=block % 2, l=l, c=c)


def to_user(x, y, h, l, c):
    return dict(x=l, y=2 * c + y % 2, h=h, l=x, c=y // 2)


def to_user_across(x, y, h, l, c):
    return dict(to_user(x, y, h, l, c), h=h + 1)


def pair_at(here, first, second):
    x, y, c = here[0], here[1], here[4]
    first, second = (x + c * (y - x) + first) % 4, (y + c * (x - y) + second) % 4
    return 4 * (first + c * (second - first)) + second + c * (first - second)


def block_at(here, first, second, s, blocks):
    return (2 * pair_at(here, first, second) + blocks - 1 + s) % blocks


def fetch(here, activations, held, sems, g, first, second, s):
    rows = held.shape[2] // 2
    block = block_at(here, first, second, s, activations.shape[1] // rows)
    return pltpu.make_async_copy(
        activations.at[:, pl.ds(pl.multiple_of(block * rows, rows), rows)],
        held.at[g, :, pl.ds(s * rows, rows)],
        sems.at[g, s],
    )


def fetch_all(groups, here, activations, held, sems):
    g = 0
    for first, second, count in groups:
        for i in range(count):
            for s in range(2):
                fetch(here, activations, held, sems, g, first, second + i, s).start()
            g += 1


def multiply_all(groups, here, cot, activations, outs, held, sems, received=()):
    rows = held.shape[2] // 2
    done = 0
    for n, (first, second, count) in enumerate(groups):
        out = outs[n // 2] if received else outs[n]
        base = 2 * (n % 2) if received else 0
        got = received[n // 2] if received and n in (0, 3) else None

        def step(i, carry, out=out, base=base, got=got, done=done, first=first, second=second):
            for s in range(2):
                fetch(here, activations, held, sems, done + i, first, second + i, s).wait()
            both = jnp.dot(cot[...], held[done + i], preferred_element_type=jnp.float32)
            for s in range(2):
                term = both[:, s * rows : (s + 1) * rows]
                if got is not None:
                    term += got[i, here[2] ^ s].astype(jnp.float32)
                out[base + i, here[2] ^ s] = term.astype(out.dtype)
            return carry

        lax.fori_loop(0, count, step, 0)
        done += count


def first_kernel(groups, here, cot_in, par_in, activations, *refs):
    cot, cot_t, par_t, *outs = refs[: 3 + len(groups)]
    held, sems, cot_raw, par_raw, raw_sems, wide = refs[3 + len(groups) :]
    raw = (
        pltpu.make_async_copy(cot_in, cot_raw, raw_sems.at[0]),
        pltpu.make_async_copy(par_in, par_raw, raw_sems.at[1]),
    )
    raw[0].start()
    fetch_all(groups, here, activations, held, sems)
    raw[1].start()
    for copy, source, plain, turned in ((raw[0], cot_raw, cot, cot_t), (raw[1], par_raw, None, par_t)):
        copy.wait()
        rows, width = source.shape[0] // 2, source.shape[1]
        wide[: 2 * rows, :] = source[...].astype(jnp.float32)
        for j in range(2):
            part = wide[pl.ds(j, rows, stride=2), :]
            at = slice(j * width, (j + 1) * width)
            if plain is not None:
                plain[:, at] = part.astype(plain.dtype)
            turned[at, :] = part.T.astype(turned.dtype)
    multiply_all(groups, here, cot_t, activations, outs, held, sems)


def first_terms(here, groups, cotangent, param_shard, activations):
    tokens, rows = cotangent.shape[0], param_shard.shape[0]
    width = cotangent.shape[2]
    total = sum(count for _, _, count in groups)
    any_space = pl.BlockSpec(memory_space=pl.ANY)
    shapes = [(tokens, 2 * width), (2 * width, tokens), (2 * width, rows)]
    shapes += [(count, 2, 2 * width, rows) for _, _, count in groups]
    return pl.pallas_call(
        functools.partial(first_kernel, groups),
        out_shape=[jax.ShapeDtypeStruct(shape, jnp.bfloat16) for shape in shapes],
        in_specs=[pl.BlockSpec(memory_space=pltpu.SMEM), any_space, any_space, any_space],
        scratch_shapes=[
            pltpu.VMEM((total, tokens, 2 * rows), jnp.bfloat16),
            pltpu.SemaphoreType.DMA((total, 2)),
            pltpu.VMEM((2 * tokens, width), jnp.bfloat16),
            pltpu.VMEM((2 * rows, width), jnp.bfloat16),
            pltpu.SemaphoreType.DMA((2,)),
            pltpu.VMEM((2 * max(tokens, rows), width), jnp.float32),
        ],
        compiler_params=MOST,
        cost_estimate=pl.CostEstimate(
            flops=8 * total * width * tokens * rows,
            bytes_accessed=4 * total * rows * (tokens + 2 * width) + 12 * width * tokens,
            transcendentals=0,
        ),
    )(here, cotangent.reshape(2 * tokens, width), param_shard.reshape(2 * rows, width), activations)


def other_kernel(groups, here, cot, activations, up_one, down_one, *refs):
    outs, held, sems = refs[:-2], refs[-2], refs[-1]
    fetch_all(groups, here, activations, held, sems)
    multiply_all(groups, here, cot, activations, outs, held, sems, (up_one, down_one))


def other_terms(here, groups, cot_t, activations, up_one, down_one, rows):
    total = sum(count for _, _, count in groups)
    columns, tokens = cot_t.shape
    in_vmem = pl.BlockSpec(memory_space=pltpu.VMEM)
    return pl.pallas_call(
        functools.partial(other_kernel, groups),
        out_shape=[
            jax.ShapeDtypeStruct((4, 2, columns, rows), jnp.bfloat16) for _ in range(len(groups) // 2)
        ],
        in_specs=[
            pl.BlockSpec(memory_space=pltpu.SMEM),
            in_vmem,
            pl.BlockSpec(memory_space=pl.ANY),
            in_vmem,
            in_vmem,
        ],
        scratch_shapes=[
            pltpu.VMEM((total, tokens, 2 * rows), jnp.bfloat16),
            pltpu.SemaphoreType.DMA((total, 2)),
        ],
        compiler_params=MOST,
        cost_estimate=pl.CostEstimate(
            flops=4 * total * columns * tokens * rows,
            bytes_accessed=4 * total * rows * (tokens + columns) + 2 * columns * tokens,
            transcendentals=0,
        ),
    )(here, cot_t, activations, up_one, down_one)


def adam_kernel(mine, theirs, master_in, first_in, second_in, sent, layer, new_master):
    grad = (mine[...].astype(jnp.float32) + theirs[...].astype(jnp.float32)).T
    rows = grad.shape[0]
    width = grad.shape[1] // 2
    for j in range(2):
        at = pl.ds(j, rows, stride=2)
        weight_grad = grad[:, j * width : (j + 1) * width]
        master = master_in[at, :]
        first = beta_one * first_in[at, :] + (1.0 - beta_one) * weight_grad
        second = beta_two * second_in[at, :] + (1.0 - beta_two) * weight_grad * weight_grad
        first_hat = first / (1.0 - beta_one**step_number)
        second_hat = second / (1.0 - beta_two**step_number)
        new_master[at, :] = master = master - learn_rate * (
            first_hat / (jnp.sqrt(second_hat) + epsilon) + decay_rate * master
        )
        sent[0, j] = first.astype(jnp.bfloat16)
        sent[1, j] = second.astype(jnp.bfloat16)
        sent[2, j] = master.astype(jnp.bfloat16)
        sent[3, j] = (master - sent[2, j].astype(jnp.float32)).astype(jnp.bfloat16)
    layer[...] = new_master[...].astype(jnp.bfloat16)


def adam(mine, theirs, master, first, second):
    rows, width = master.shape
    return pl.pallas_call(
        adam_kernel,
        out_shape=(
            jax.ShapeDtypeStruct((4, 2, rows // 2, width), jnp.bfloat16),
            jax.ShapeDtypeStruct((rows, width), jnp.bfloat16),
        ),
        scratch_shapes=[pltpu.VMEM((rows, width), jnp.float32)],
        compiler_params=WIDE,
        cost_estimate=pl.CostEstimate(
            flops=20 * rows * width, bytes_accessed=30 * rows * width, transcendentals=2 * rows * width
        ),
    )(mine, theirs, master, first, second)


def place_kernel(groups, here, *refs):
    sources, out, sems = refs[: len(groups)], refs[-2], refs[-1]
    copies = []
    for source, (first, second) in zip(sources, groups):
        for i in range(source.shape[0]):
            for s in range(2):
                at = block_at(here, first, second + i, s, out.shape[0])
                copies.append(pltpu.make_async_copy(source.at[i, s], out.at[at], sems.at[len(copies)]))
    for copy in copies:
        copy.start()
    for copy in copies:
        copy.wait()


def place(here, groups, sources, total, into=None):
    block = sources[0].shape[2:]
    held = [] if into is None else [into]
    count = 2 * sum(source.shape[0] for source in sources)
    any_space = pl.BlockSpec(memory_space=pl.ANY)
    return pl.pallas_call(
        functools.partial(place_kernel, groups),
        out_shape=jax.ShapeDtypeStruct((total,) + block, sources[0].dtype),
        in_specs=[pl.BlockSpec(memory_space=pltpu.SMEM)]
        + [pl.BlockSpec(memory_space=pltpu.VMEM)] * len(sources)
        + [any_space] * len(held),
        out_specs=any_space,
        scratch_shapes=[pltpu.SemaphoreType.DMA((count,))],
        input_output_aliases={} if into is None else {1 + len(sources): 0},
        compiler_params=WIDE,
        cost_estimate=pl.CostEstimate(flops=0, bytes_accessed=0, transcendentals=0),
    )(here, *sources, *held)


def unpack_kernel(sent, master, first, second):
    rows = sent.shape[2]
    for j in range(2):
        at = pl.ds(j, rows, stride=2)
        first[at, :] = sent[0, j].astype(jnp.float32)
        second[at, :] = sent[1, j].astype(jnp.float32)
        master[at, :] = sent[2, j].astype(jnp.float32) + sent[3, j].astype(jnp.float32)


def unpack(sent):
    _, _, rows, width = sent.shape
    return pl.pallas_call(
        unpack_kernel,
        out_shape=[jax.ShapeDtypeStruct((2 * rows, width), jnp.float32)] * 3,
        compiler_params=WIDE,
        cost_estimate=pl.CostEstimate(flops=0, bytes_accessed=10 * sent.size, transcendentals=0),
    )(sent)


def input_kernel(here, cot_mine, cot_theirs, params, out, total):
    step = pl.program_id(0)
    rows = params.shape[3]
    c = here[4]

    @pl.when(step == 0)
    def _():
        total[...] = jnp.zeros_like(total)

    for part in range(2):
        for s in range(2):
            at = slice((2 * part + s) * rows, (2 * part + s + 1) * rows)
            total[:, at] += jnp.dot(
                cot_mine[0], params[2 * c + part, s], preferred_element_type=jnp.float32
            ) + jnp.dot(cot_theirs[0], params[2 - 2 * c + part, s], preferred_element_type=jnp.float32)

    @pl.when(step == pl.num_programs(0) - 1)
    def _():
        out[...] = total[...].astype(out.dtype)


def input_matmul(here, cot_mine, cot_theirs, params):
    chips, tokens, columns = cot_mine.shape
    rows = params.shape[3]
    cot_spec = pl.BlockSpec((1, tokens, columns), lambda k, here: (k, 0, 0))
    return pl.pallas_call(
        input_kernel,
        out_shape=jax.ShapeDtypeStruct((tokens, 4 * rows), jnp.bfloat16),
        grid_spec=pltpu.PrefetchScalarGridSpec(
            num_scalar_prefetch=1,
            grid=(chips,),
            in_specs=[
                cot_spec,
                cot_spec,
                pl.BlockSpec((4, 2, columns, rows), lambda k, here: ((here[3] + 4 - k) % 4, 0, 0, 0)),
            ],
            out_specs=pl.BlockSpec((tokens, 4 * rows), lambda k, here: (0, 0)),
            scratch_shapes=[pltpu.VMEM((tokens, 4 * rows), jnp.float32)],
        ),
        compiler_params=MOST,
        cost_estimate=pl.CostEstimate(
            flops=16 * chips * tokens * columns * rows,
            bytes_accessed=4 * chips * columns * (tokens + 2 * rows) + 8 * tokens * rows,
            transcendentals=0,
        ),
    )(here, cot_mine, cot_theirs, params)


def add(*terms):
    total = terms[0].astype(jnp.float32)
    for term in terms[1:]:
        total = total + term.astype(jnp.float32)
    return total.astype(jnp.bfloat16)


def tie(*values):
    return lax.optimization_barrier(values)


def per_device(activations, cotangent, param_shard, master_store, first_store, second_store):
    x, y, h, l, c = (lax.axis_index(a) for a in AXES)
    tokens, _, width = cotangent.shape
    rows = param_shard.shape[0]
    columns = 2 * width
    here = jnp.stack([x, y, h, l, c]).astype(jnp.int32)

    flat_cot, cot_t, par, up, down = first_terms(
        here, ((2, 0, 2), (2, 2, 2)), cotangent, param_shard, activations
    )
    up_one, down_one = move(up, along_first(1)), move(down, along_first(-1))
    par_same, par_other = move(par, to_user), move(par, to_user_across)
    cots = [flat_cot, move(flat_cot, next_in_line)]
    up, down, own = other_terms(
        here,
        ((1, 0, 2), (1, 2, 2), (3, 0, 2), (3, 2, 2), (0, 0, 2), (0, 2, 2)),
        cot_t,
        activations,
        up_one,
        down_one,
        rows,
    )
    up, down, par_same, par_other, cots[1] = tie(up, down, par_same, par_other, cots[1])
    up_two, down_two = move(up, along_first(1)), move(down, along_first(-1))
    pair = jnp.where(h == 0, jnp.stack([par_same, par_other]), jnp.stack([par_other, par_same]))
    params = lax.all_gather(pair, ("x", "y"), axis=0)
    cots += [move(cots[1], next_in_line), move(flat_cot, back_in_line)]
    sums = [add(own[i], up_two[i], down_two[i]) for i in range(4)]

    sums[1], sums[2], sums[3], cots[2], cots[3] = tie(*sums[1:], cots[2], cots[3])
    cot_mine = jnp.stack(cots)
    cot_theirs = move(cot_mine, other_core)
    got = [
        move(sums[1], along_second(1)),
        move(sums[3], along_second(-1)),
        move(sums[2], along_second(2)),
    ]
    far = add(sums[0][1], *(g[1] for g in got))
    near = add(sums[0][0], *(g[0] for g in got))
    far, cot_theirs = tie(far, cot_theirs)
    state = [v.reshape(2 * rows, width) for v in (master_store, first_store, second_store)]
    sent, layer = adam(near, move(far, other_half), *state)

    layer_other = move(layer, other_half)
    pair = jnp.where(h == 0, jnp.stack([layer, layer_other]), jnp.stack([layer_other, layer]))
    from_up = move(pair, along_second(-1))
    from_down = move(pair, along_second(1))
    from_far = move(pair, along_second(2))
    low, high = jnp.stack([pair, from_up]), jnp.stack([from_far, from_down])
    low, high, sent = tie(low, high, sent)
    low_down, high_up = move(low, along_first(1)), move(high, along_first(-1))
    high_down, low_up = move(high, along_first(1)), move(low, along_first(-1))
    sent = move(sent, previous_block)
    low_down, high_up = tie(low_down, high_up)
    low_far, high_far = move(low_down, along_first(1)), move(high_up, along_first(-1))
    input_grad = input_matmul(here, cot_mine, cot_theirs, params)
    low_up, high_down, input_grad = tie(low_up, high_down, input_grad)
    new_layer = place(
        here,
        ((0, 0), (0, 2), (1, 0), (1, 2), (-1, 0), (-1, 2)),
        [low, high, low_up, high_up, low_down, high_down],
        32,
    )
    new_layer, sent = tie(new_layer, sent)
    new_layer, *state = tie(new_layer, *unpack(sent))
    new_layer = place(here, ((2, 0), (2, 2)), [low_far, high_far], 32, new_layer)
    new_master, new_first, new_second = (v.reshape(rows, 2, width) for v in state)
    return (
        input_grad,
        new_master,
        new_first,
        new_second,
        new_layer.reshape(32 * rows, 2, width),
    )


def solution(mesh):
    fine = Mesh(mesh.devices.reshape(tuple(SIZES.values())), AXES)
    return jax.shard_map(
        per_device,
        mesh=fine,
        in_specs=(
            P(DP, None),
            P(DP, None, MP),
            P(DP, None, MP),
            P(DP, None, MP),
            P(DP, None, MP),
            P(DP, None, MP),
        ),
        out_specs=(
            P(DP, MP),
            P(DP, None, MP),
            P(DP, None, MP),
            P(DP, None, MP),
            P(None, None, MP),
        ),
        check_vma=False,
    )
```

```python
import functools

import jax
import jax.numpy as jnp
import numpy as np
from jax import lax
from jax.experimental import pallas as pl
from jax.experimental.pallas import tpu as pltpu
from jax.sharding import Mesh, PartitionSpec as P

learn_rate = 0.001
beta_one = 0.9
beta_two = 0.95
decay_rate = 0.1
epsilon = 1e-08
step_number = 10

SIZES = {"x": 4, "y": 4, "h": 2, "l": 4, "c": 2}
AXES = tuple(SIZES)
DP = ("x", "y", "h")
MP = ("l", "c")
MOST = pltpu.CompilerParams(vmem_limit_bytes=56 * 2**20)
WIDE = pltpu.CompilerParams(vmem_limit_bytes=32 * 2**20)


def move(value, target):
    shape = tuple(SIZES.values())
    pairs = []
    for source in range(int(np.prod(shape))):
        at = dict(zip(AXES, (int(i) for i in np.unravel_index(source, shape))))
        to = target(**at)
        pairs.append((source, int(np.ravel_multi_index([to[a] % SIZES[a] for a in AXES], shape))))
    return lax.ppermute(value, AXES, pairs)


def along_first(by):
    def target(x, y, h, l, c):
        return dict(x=x + by * (1 - c), y=y + by * c, h=h, l=l, c=c)

    return target


def along_second(by):
    def target(x, y, h, l, c):
        return dict(x=x + by * c, y=y + by * (1 - c), h=h, l=l, c=c)

    return target


def other_half(x, y, h, l, c):
    return dict(x=x, y=y, h=h + 1, l=l, c=c)


def other_core(x, y, h, l, c):
    return dict(x=x, y=y, h=h, l=l, c=c + 1)


def next_in_line(x, y, h, l, c):
    return dict(x=x, y=y, h=h, l=l + 1, c=c)


def back_in_line(x, y, h, l, c):
    return dict(x=x, y=y, h=h, l=l - 1, c=c)


def previous_block(x, y, h, l, c):
    block = (x * 8 + y * 2 + h - 1) % 32
    return dict(x=block // 8, y=block // 2 % 4, h=block % 2, l=l, c=c)


def to_user(x, y, h, l, c):
    return dict(x=l, y=2 * c + y % 2, h=h, l=x, c=y // 2)


def to_user_across(x, y, h, l, c):
    return dict(to_user(x, y, h, l, c), h=h + 1)


def pair_at(here, first, second):
    x, y, c = here[0], here[1], here[4]
    first, second = (x + c * (y - x) + first) % 4, (y + c * (x - y) + second) % 4
    return 4 * (first + c * (second - first)) + second + c * (first - second)


def block_at(here, first, second, s, blocks):
    return (2 * pair_at(here, first, second) + blocks - 1 + s) % blocks


def fetch(here, activations, held, sems, g, first, second, s):
    rows = held.shape[2] // 2
    block = block_at(here, first, second, s, activations.shape[1] // rows)
    return pltpu.make_async_copy(
        activations.at[:, pl.ds(pl.multiple_of(block * rows, rows), rows)],
        held.at[g, :, pl.ds(s * rows, rows)],
        sems.at[g, s],
    )


def fetch_all(groups, here, activations, held, sems):
    g = 0
    for first, second, count in groups:
        for i in range(count):
            for s in range(2):
                fetch(here, activations, held, sems, g, first, second + i, s).start()
            g += 1


def multiply_all(groups, here, cot, activations, outs, held, sems, received=()):
    rows = held.shape[2] // 2
    done = 0
    for n, (first, second, count) in enumerate(groups):
        out = outs[n // 2] if received else outs[n]
        base = 2 * (n % 2) if received else 0
        got = received[n // 2] if received and n in (0, 3) else None

        def step(i, carry, out=out, base=base, got=got, done=done, first=first, second=second):
            for s in range(2):
                fetch(here, activations, held, sems, done + i, first, second + i, s).wait()
            both = jnp.dot(cot[...], held[done + i], preferred_element_type=jnp.float32)
            for s in range(2):
                term = both[:, s * rows : (s + 1) * rows]
                if got is not None:
                    term += got[i, here[2] ^ s].astype(jnp.float32)
                out[base + i, here[2] ^ s] = term.astype(out.dtype)
            return carry

        lax.fori_loop(0, count, step, 0)
        done += count


def first_kernel(groups, here, cot_in, par_in, activations, *refs):
    cot, cot_t, par_t, *outs = refs[: 3 + len(groups)]
    held, sems, cot_raw, par_raw, raw_sems, wide = refs[3 + len(groups) :]
    raw = (
        pltpu.make_async_copy(cot_in, cot_raw, raw_sems.at[0]),
        pltpu.make_async_copy(par_in, par_raw, raw_sems.at[1]),
    )
    raw[0].start()
    fetch_all(groups, here, activations, held, sems)
    raw[1].start()
    for copy, source, plain, turned in ((raw[0], cot_raw, cot, cot_t), (raw[1], par_raw, None, par_t)):
        copy.wait()
        rows, width = source.shape[0] // 2, source.shape[1]
        wide[: 2 * rows, :] = source[...].astype(jnp.float32)
        for j in range(2):
            part = wide[pl.ds(j, rows, stride=2), :]
            at = slice(j * width, (j + 1) * width)
            if plain is not None:
                plain[:, at] = part.astype(plain.dtype)
            turned[at, :] = part.T.astype(turned.dtype)
    multiply_all(groups, here, cot_t, activations, outs, held, sems)


def first_terms(here, groups, cotangent, param_shard, activations):
    tokens, rows = cotangent.shape[0], param_shard.shape[0]
    width = cotangent.shape[2]
    total = sum(count for _, _, count in groups)
    any_space = pl.BlockSpec(memory_space=pl.ANY)
    shapes = [(tokens, 2 * width), (2 * width, tokens), (2 * width, rows)]
    shapes += [(count, 2, 2 * width, rows) for _, _, count in groups]
    return pl.pallas_call(
        functools.partial(first_kernel, groups),
        out_shape=[jax.ShapeDtypeStruct(shape, jnp.bfloat16) for shape in shapes],
        in_specs=[pl.BlockSpec(memory_space=pltpu.SMEM), any_space, any_space, any_space],
        scratch_shapes=[
            pltpu.VMEM((total, tokens, 2 * rows), jnp.bfloat16),
            pltpu.SemaphoreType.DMA((total, 2)),
            pltpu.VMEM((2 * tokens, width), jnp.bfloat16),
            pltpu.VMEM((2 * rows, width), jnp.bfloat16),
            pltpu.SemaphoreType.DMA((2,)),
            pltpu.VMEM((2 * max(tokens, rows), width), jnp.float32),
        ],
        compiler_params=MOST,
        cost_estimate=pl.CostEstimate(
            flops=8 * total * width * tokens * rows,
            bytes_accessed=4 * total * rows * (tokens + 2 * width) + 12 * width * tokens,
            transcendentals=0,
        ),
    )(here, cotangent.reshape(2 * tokens, width), param_shard.reshape(2 * rows, width), activations)


def other_kernel(groups, here, cot, activations, up_one, down_one, *refs):
    outs, held, sems = refs[:-2], refs[-2], refs[-1]
    fetch_all(groups, here, activations, held, sems)
    multiply_all(groups, here, cot, activations, outs, held, sems, (up_one, down_one))


def other_terms(here, groups, cot_t, activations, up_one, down_one, rows):
    total = sum(count for _, _, count in groups)
    columns, tokens = cot_t.shape
    in_vmem = pl.BlockSpec(memory_space=pltpu.VMEM)
    return pl.pallas_call(
        functools.partial(other_kernel, groups),
        out_shape=[
            jax.ShapeDtypeStruct((4, 2, columns, rows), jnp.bfloat16) for _ in range(len(groups) // 2)
        ],
        in_specs=[
            pl.BlockSpec(memory_space=pltpu.SMEM),
            in_vmem,
            pl.BlockSpec(memory_space=pl.ANY),
            in_vmem,
            in_vmem,
        ],
        scratch_shapes=[
            pltpu.VMEM((total, tokens, 2 * rows), jnp.bfloat16),
            pltpu.SemaphoreType.DMA((total, 2)),
        ],
        compiler_params=MOST,
        cost_estimate=pl.CostEstimate(
            flops=4 * total * columns * tokens * rows,
            bytes_accessed=4 * total * rows * (tokens + columns) + 2 * columns * tokens,
            transcendentals=0,
        ),
    )(here, cot_t, activations, up_one, down_one)


def adam_kernel(mine, theirs, master_in, first_in, second_in, sent, layer, new_master):
    grad = (mine[...].astype(jnp.float32) + theirs[...].astype(jnp.float32)).T
    rows = grad.shape[0]
    width = grad.shape[1] // 2
    for j in range(2):
        at = pl.ds(j, rows, stride=2)
        weight_grad = grad[:, j * width : (j + 1) * width]
        master = master_in[at, :]
        first = beta_one * first_in[at, :] + (1.0 - beta_one) * weight_grad
        second = beta_two * second_in[at, :] + (1.0 - beta_two) * weight_grad * weight_grad
        first_hat = first / (1.0 - beta_one**step_number)
        second_hat = second / (1.0 - beta_two**step_number)
        new_master[at, :] = master = master - learn_rate * (
            first_hat / (jnp.sqrt(second_hat) + epsilon) + decay_rate * master
        )
        sent[0, j] = first.astype(jnp.bfloat16)
        sent[1, j] = second.astype(jnp.bfloat16)
        sent[2, j] = master.astype(jnp.bfloat16)
        sent[3, j] = (master - sent[2, j].astype(jnp.float32)).astype(jnp.bfloat16)
    layer[...] = new_master[...].astype(jnp.bfloat16)


def adam(mine, theirs, master, first, second):
    rows, width = master.shape
    return pl.pallas_call(
        adam_kernel,
        out_shape=(
            jax.ShapeDtypeStruct((4, 2, rows // 2, width), jnp.bfloat16),
            jax.ShapeDtypeStruct((rows, width), jnp.bfloat16),
        ),
        scratch_shapes=[pltpu.VMEM((rows, width), jnp.float32)],
        compiler_params=WIDE,
        cost_estimate=pl.CostEstimate(
            flops=20 * rows * width, bytes_accessed=30 * rows * width, transcendentals=2 * rows * width
        ),
    )(mine, theirs, master, first, second)


def place_kernel(groups, here, *refs):
    sources, out, sems = refs[: len(groups)], refs[-2], refs[-1]
    copies = []
    for source, (first, second) in zip(sources, groups):
        for i in range(source.shape[0]):
            for s in range(2):
                at = block_at(here, first, second + i, s, out.shape[0])
                copies.append(pltpu.make_async_copy(source.at[i, s], out.at[at], sems.at[len(copies)]))
    for copy in copies:
        copy.start()
    for copy in copies:
        copy.wait()


def place(here, groups, sources, total, into=None):
    block = sources[0].shape[2:]
    held = [] if into is None else [into]
    count = 2 * sum(source.shape[0] for source in sources)
    any_space = pl.BlockSpec(memory_space=pl.ANY)
    return pl.pallas_call(
        functools.partial(place_kernel, groups),
        out_shape=jax.ShapeDtypeStruct((total,) + block, sources[0].dtype),
        in_specs=[pl.BlockSpec(memory_space=pltpu.SMEM)]
        + [pl.BlockSpec(memory_space=pltpu.VMEM)] * len(sources)
        + [any_space] * len(held),
        out_specs=any_space,
        scratch_shapes=[pltpu.SemaphoreType.DMA((count,))],
        input_output_aliases={} if into is None else {1 + len(sources): 0},
        compiler_params=WIDE,
        cost_estimate=pl.CostEstimate(flops=0, bytes_accessed=0, transcendentals=0),
    )(here, *sources, *held)


def unpack_kernel(sent, master, first, second):
    rows = sent.shape[2]
    for j in range(2):
        at = pl.ds(j, rows, stride=2)
        first[at, :] = sent[0, j].astype(jnp.float32)
        second[at, :] = sent[1, j].astype(jnp.float32)
        master[at, :] = sent[2, j].astype(jnp.float32) + sent[3, j].astype(jnp.float32)


def unpack(sent):
    _, _, rows, width = sent.shape
    return pl.pallas_call(
        unpack_kernel,
        out_shape=[jax.ShapeDtypeStruct((2 * rows, width), jnp.float32)] * 3,
        compiler_params=WIDE,
        cost_estimate=pl.CostEstimate(flops=0, bytes_accessed=10 * sent.size, transcendentals=0),
    )(sent)


def input_kernel(here, cot_mine, cot_theirs, params, out, total):
    step = pl.program_id(0)
    rows = params.shape[3]
    c = here[4]

    @pl.when(step == 0)
    def _():
        total[...] = jnp.zeros_like(total)

    for part in range(2):
        for s in range(2):
            at = slice((2 * part + s) * rows, (2 * part + s + 1) * rows)
            total[:, at] += jnp.dot(
                cot_mine[0], params[2 * c + part, s], preferred_element_type=jnp.float32
            ) + jnp.dot(cot_theirs[0], params[2 - 2 * c + part, s], preferred_element_type=jnp.float32)

    @pl.when(step == pl.num_programs(0) - 1)
    def _():
        out[...] = total[...].astype(out.dtype)


def input_matmul(here, cot_mine, cot_theirs, params):
    chips, tokens, columns = cot_mine.shape
    rows = params.shape[3]
    cot_spec = pl.BlockSpec((1, tokens, columns), lambda k, here: (k, 0, 0))
    return pl.pallas_call(
        input_kernel,
        out_shape=jax.ShapeDtypeStruct((tokens, 4 * rows), jnp.bfloat16),
        grid_spec=pltpu.PrefetchScalarGridSpec(
            num_scalar_prefetch=1,
            grid=(chips,),
            in_specs=[
                cot_spec,
                cot_spec,
                pl.BlockSpec((4, 2, columns, rows), lambda k, here: ((here[3] + 4 - k) % 4, 0, 0, 0)),
            ],
            out_specs=pl.BlockSpec((tokens, 4 * rows), lambda k, here: (0, 0)),
            scratch_shapes=[pltpu.VMEM((tokens, 4 * rows), jnp.float32)],
        ),
        compiler_params=MOST,
        cost_estimate=pl.CostEstimate(
            flops=16 * chips * tokens * columns * rows,
            bytes_accessed=4 * chips * columns * (tokens + 2 * rows) + 8 * tokens * rows,
            transcendentals=0,
        ),
    )(here, cot_mine, cot_theirs, params)


def add(*terms):
    total = terms[0].astype(jnp.float32)
    for term in terms[1:]:
        total = total + term.astype(jnp.float32)
    return total.astype(jnp.bfloat16)


def tie(*values):
    return lax.optimization_barrier(values)


def per_device(activations, cotangent, param_shard, master_store, first_store, second_store):
    x, y, h, l, c = (lax.axis_index(a) for a in AXES)
    tokens, _, width = cotangent.shape
    rows = param_shard.shape[0]
    columns = 2 * width
    here = jnp.stack([x, y, h, l, c]).astype(jnp.int32)

    flat_cot, cot_t, par, up, down = first_terms(
        here, ((2, 0, 2), (2, 2, 2)), cotangent, param_shard, activations
    )
    up_one, down_one = move(up, along_first(1)), move(down, along_first(-1))
    par_same, par_other = move(par, to_user), move(par, to_user_across)
    cots = [flat_cot, move(flat_cot, next_in_line)]
    up, down, own = other_terms(
        here,
        ((1, 0, 2), (1, 2, 2), (3, 0, 2), (3, 2, 2), (0, 0, 2), (0, 2, 2)),
        cot_t,
        activations,
        up_one,
        down_one,
        rows,
    )
    up, down, par_same, par_other, cots[1] = tie(up, down, par_same, par_other, cots[1])
    up_two, down_two = move(up, along_first(1)), move(down, along_first(-1))
    pair = jnp.where(h == 0, jnp.stack([par_same, par_other]), jnp.stack([par_other, par_same]))
    params = lax.all_gather(pair, ("x", "y"), axis=0)
    cots += [move(cots[1], next_in_line), move(flat_cot, back_in_line)]
    sums = [add(own[i], up_two[i], down_two[i]) for i in range(4)]

    sums[1], sums[2], sums[3], cots[2], cots[3] = tie(*sums[1:], cots[2], cots[3])
    cot_mine = jnp.stack(cots)
    cot_theirs = move(cot_mine, other_core)
    got = [
        move(sums[1], along_second(1)),
        move(sums[3], along_second(-1)),
        move(sums[2], along_second(2)),
    ]
    far = add(sums[0][1], *(g[1] for g in got))
    near = add(sums[0][0], *(g[0] for g in got))
    far, cot_theirs = tie(far, cot_theirs)
    state = [v.reshape(2 * rows, width) for v in (master_store, first_store, second_store)]
    sent, layer = adam(near, move(far, other_half), *state)

    layer_other, sent = tie(move(layer, other_half), sent)
    sent = move(sent, previous_block)
    pair = jnp.where(h == 0, jnp.stack([layer, layer_other]), jnp.stack([layer_other, layer]))
    from_up = move(pair, along_second(-1))
    from_down = move(pair, along_second(1))
    from_far = move(pair, along_second(2))
    low, high = jnp.stack([pair, from_up]), jnp.stack([from_far, from_down])
    low, high = tie(low, high)
    low_down, high_up = move(low, along_first(1)), move(high, along_first(-1))
    high_down, low_up = move(high, along_first(1)), move(low, along_first(-1))
    low_down, high_up, sent = tie(low_down, high_up, sent)
    low_far, high_far = move(low_down, along_first(1)), move(high_up, along_first(-1))
    input_grad = input_matmul(here, cot_mine, cot_theirs, params)
    low_up, high_down, input_grad = tie(low_up, high_down, input_grad)
    new_layer = place(
        here,
        ((0, 0), (0, 2), (1, 0), (1, 2), (-1, 0), (-1, 2)),
        [low, high, low_up, high_up, low_down, high_down],
        32,
    )
    new_layer, *state = tie(new_layer, *unpack(sent))
    new_layer = place(here, ((2, 0), (2, 2)), [low_far, high_far], 32, new_layer)
    new_master, new_first, new_second = (v.reshape(rows, 2, width) for v in state)
    return (
        input_grad,
        new_master,
        new_first,
        new_second,
        new_layer.reshape(32 * rows, 2, width),
    )


def solution(mesh):
    fine = Mesh(mesh.devices.reshape(tuple(SIZES.values())), AXES)
    return jax.shard_map(
        per_device,
        mesh=fine,
        in_specs=(
            P(DP, None),
            P(DP, None, MP),
            P(DP, None, MP),
            P(DP, None, MP),
            P(DP, None, MP),
            P(DP, None, MP),
        ),
        out_specs=(
            P(DP, MP),
            P(DP, None, MP),
            P(DP, None, MP),
            P(DP, None, MP),
            P(None, None, MP),
        ),
        check_vma=False,
    )
```
